128 devices in a mesh: row: 8 (over y, core), col: 16 (over z, x).
Axes of the slice: x: 4, y: 4, z: 4, core: 2. Of those that a mesh axis runs over, the one named last changes fastest.
Arguments:
- basis_values: bfloat16 [128, 1024, 2048], P(('row', 'col')), may hold values from -6 to 6
- grid_weights: float32 [128, 1024], P(('row', 'col')), may hold values from 0.005 to 0.1
- density_tiles: bfloat16 [16384, 128, 128], P(('row', 'col')), may hold values from -0.125 to 0.125
- tile_index: int32 [128, 256], P(('row', 'col')), may hold values from 0 to 16383, as said below
Outputs:
- potential_tiles: float32 [16384, 128, 128], P(('row', 'col'))
- grid_density: float32 [128, 1024], P(('row', 'col'))
The draws below stay inside these ranges and needn't reach their ends.
Inputs may be any that keep to these rules, and one draw needn't show every extreme that they name: `tile_index`: within one region the 256 entries are distinct. An entry divided by 128 (rounded down) is the index, rows major, of the device storing that tile. One region names at most 4 tiles stored on one device, and one device is named exactly 4 times by every region.
All inputs are finite; a program needn't handle non-finite values.
Results may differ from the reference program's by a relative error of at most 0.0041.
Values may be sent and summed in bfloat16 or wider, within the bound.
No kernel may reach another device: no remote copies, remote signals or barrier semaphores. Data moves between devices by JAX's collectives and lax.ppermute only.
A program may use at most 128 MiB of HBM per device.

```python
import math
import jax
import jax.numpy as jnp
from jax import lax

TILE = 128
SIG = 16
PTS = 1024
NNZ_DEV = 128
REGIONS = 128
NNZ = 16384
CAP = 4
N_ROW = 8
N_COL = 16


def draw_tile_index(key, part):
    key = jax.random.fold_in(key, 7)
    count = N_ROW * N_COL
    slots = count * CAP
    hot_key, region_key = jax.random.split(key)
    order = jax.random.permutation(hot_key, count).astype(jnp.int32)
    place = jnp.zeros((count,), jnp.int32).at[order].set(jnp.arange(count, dtype=jnp.int32))
    first_owner = order[0]
    bucket = jnp.arange(slots, dtype=jnp.int32) // CAP
    is_first = bucket == first_owner
    is_hot = place[bucket] < max(count // 8, 1)

    def one_region(single_key):
        rank_key, shift_key, mix_key = jax.random.split(single_key, 3)
        rank = jax.random.permutation(rank_key, slots).astype(jnp.int32)
        score = jnp.where(is_first, rank - 2 * slots, jnp.where(is_hot, rank // 4, rank))
        chosen = jnp.argsort(score, stable=True)[:SIG * SIG].astype(jnp.int32)
        chosen = chosen[jax.random.permutation(mix_key, SIG * SIG)]
        owner_of = chosen // CAP
        within = chosen % CAP
        shifts = jax.random.randint(shift_key, (count,), 0, NNZ_DEV).astype(jnp.int32)
        return (owner_of * NNZ_DEV + (within + shifts[owner_of]) % NNZ_DEV).astype(jnp.int32)
    return jax.vmap(one_region)(jax.random.split(region_key, REGIONS))


def steps_of(own_key, shape, cuts, low, top_value):
    loudness = 1.0
    for dim, shards_of in cuts:
        steps = jax.random.uniform(jax.random.fold_in(jax.random.fold_in(own_key, 6), dim), (shards_of,), jnp.float32, low / len(cuts), top_value / len(cuts))
        loudness = loudness * jnp.repeat(jnp.exp(steps), shape[dim] // shards_of).reshape((-1,) + (1,) * (len(shape) - 1 - dim))
    return loudness


def centred(own_key, dims, deviation, bound, cuts=(), kind=jnp.bfloat16):
    factor_of = steps_of(own_key, dims, cuts, -0.22, 0.18) if cuts else 1.0
    array = jax.random.normal(own_key, dims, jnp.float32) * deviation * factor_of
    return jnp.minimum(jnp.maximum(array, -bound), bound).astype(kind)


def setup_inputs(seed: int = 0) -> dict:
    key_list = jax.random.split(jax.random.key(seed), 5)
    return {
        "basis_values": centred(key_list[0], (REGIONS, PTS, SIG * TILE), 1.0, 6.0, ((0, 128),)),
        "grid_weights": jnp.clip(jnp.exp(math.log(0.1) - 2.9957323 * jax.random.uniform(key_list[1], (REGIONS, PTS), jnp.float32) ** steps_of(key_list[1], (REGIONS, PTS), ((0, 128),), -0.2, 0.2)), 0.005, 0.1),
        "density_tiles": centred(key_list[2], (NNZ, TILE, TILE), (SIG * TILE) ** -0.5, 0.125, ((0, 128),)),
        "tile_index": draw_tile_index(jax.random.fold_in(key_list[4], 71), 0),
    }


exchange_coeff = 0.98474502184269641


def reference(basis_values, grid_weights, density_tiles, tile_index):
    def one_region(carry, inputs):
        values_r, weights_r, index_r = inputs
        tiles = density_tiles[index_r].astype(jnp.float32).reshape(SIG, SIG, TILE, TILE)
        values = values_r.astype(jnp.float32).reshape(PTS, SIG, TILE)
        mixed = jnp.einsum("npi,pqij->nqj", values, tiles, precision=lax.Precision.HIGHEST)
        density = jnp.sum(mixed * values, axis=(1, 2))
        weighted = -exchange_coeff * weights_r * density / (density * density + 1.0) ** (1.0 / 3.0)
        scaled = (weighted[:, None, None] * values).astype(jnp.bfloat16)
        partial_tiles = jnp.einsum("npi,nqj->pqij", values, scaled.astype(jnp.float32), precision=lax.Precision.HIGHEST)
        rounded = lax.optimization_barrier(partial_tiles.astype(jnp.bfloat16))
        carry = carry.at[index_r].add(rounded.astype(jnp.float32).reshape(SIG * SIG, TILE, TILE))
        return carry, density

    start = jnp.zeros((NNZ, TILE, TILE), jnp.float32)
    potential_tiles, grid_density = lax.scan(one_region, start, (basis_values, grid_weights, tile_index))
    return potential_tiles, grid_density
```

```python
import functools

import jax
import jax.numpy as jnp
from jax import lax
from jax.experimental import pallas as pl
from jax.experimental.pallas import tpu as pltpu
from jax.sharding import PartitionSpec as P

exchange_coeff = 0.9847450218426964
AXES = ("row", "col")
VMEM_BYTES = 56 * 1024 * 1024


def fetch_kernel(asked_ref, tiles_ref, out_ref, sem):
    slots = out_ref.shape[0]

    def start(step, carry):
        for lane in range(8):
            slot = step * 8 + lane
            tile = jnp.maximum(asked_ref[slot], 0)
            pltpu.make_async_copy(tiles_ref.at[tile], out_ref.at[slot], sem).start()
        return carry

    lax.fori_loop(0, slots // 8, start, 0)
    pltpu.make_async_copy(out_ref, out_ref, sem).wait()


def region_kernel(
    slot_ref, values_ref, turned_ref, weights_ref, reply_ref, out_ref, density_ref,
    block, scaled, partial, load_sems, store_sem,
):
    points, width_all = values_ref.shape
    width = reply_ref.shape[1]
    sig = width_all // width
    chunk = 2 * width
    chunks = width_all // chunk

    def start_chunk(j):
        def body(p, carry):
            for half in range(2):
                q = 2 * j + half
                slot = slot_ref[p * sig + q]
                pltpu.make_async_copy(
                    reply_ref.at[slot],
                    block.at[pl.ds(pl.multiple_of(p * width, width), width), pl.ds(q * width, width)],
                    load_sems.at[j],
                ).start()
            return carry

        lax.fori_loop(0, sig, body, 0)

    for j in range(chunks):
        start_chunk(j)
    total = jnp.zeros((points, width), jnp.float32)
    for j in range(chunks):
        columns = block.at[:, pl.ds(j * chunk, chunk)]
        pltpu.make_async_copy(columns, columns, load_sems.at[j]).wait()
        mixed = jnp.dot(values_ref[...], columns[...], preferred_element_type=jnp.float32)
        product = mixed * values_ref[:, pl.ds(j * chunk, chunk)].astype(jnp.float32)
        total = total + product[:, :width] + product[:, width:]
    density = jnp.sum(total, axis=1, keepdims=True)
    density = jnp.broadcast_to(density, (points, width))
    density_ref[...] = density.T[:1, :]
    weights = jnp.broadcast_to(weights_ref[...], (width, points)).T
    cube_root = jnp.exp(jnp.log(density * density + 1.0) * (1.0 / 3.0))
    weighted = -exchange_coeff * weights * density / cube_root
    for q in range(sig):
        columns = pl.ds(q * width, width)
        scaled[:, columns] = (weighted * values_ref[:, columns].astype(jnp.float32)).astype(jnp.bfloat16)
    for i in range(chunks):
        rows = pl.ds(i * chunk, chunk)
        partial[rows, :] = jnp.dot(
            turned_ref[rows, :], scaled[...], preferred_element_type=jnp.float32
        ).astype(jnp.bfloat16)

        def store(q, carry):
            for half in range(2):
                p = 2 * i + half
                pltpu.make_async_copy(
                    partial.at[pl.ds(p * width, width), pl.ds(pl.multiple_of(q * width, width), width)],
                    out_ref.at[slot_ref[p * sig + q]],
                    store_sem,
                ).start()
            return carry

        lax.fori_loop(0, sig, store, 0)
    pltpu.make_async_copy(partial, partial, store_sem).wait()


def collect_kernel(asked_ref, arrived_ref, out_ref, held, sems):
    slots = arrived_ref.shape[0]
    parts = sems.shape[0]
    size = slots // parts

    def piece(j):
        return pltpu.make_async_copy(
            arrived_ref.at[pl.ds(j * size, size)], held.at[pl.ds(j * size, size)], sems.at[j]
        )

    for j in range(parts):
        piece(j).start()
    out_ref[...] = jnp.zeros_like(out_ref)

    def add(slot, carry):
        tile = asked_ref[slot]

        @pl.when(tile >= 0)
        def _():
            out_ref[tile] = out_ref[tile] + held[slot].astype(jnp.float32)

        return carry

    for j in range(parts):
        piece(j).wait()
        lax.fori_loop(j * size, (j + 1) * size, add, 0)


def fetch(asked, tiles):
    slots = asked.shape[0]
    return pl.pallas_call(
        fetch_kernel,
        out_shape=jax.ShapeDtypeStruct((slots,) + tiles.shape[1:], tiles.dtype),
        in_specs=[pl.BlockSpec(memory_space=pltpu.SMEM), pl.BlockSpec(memory_space=pltpu.VMEM)],
        out_specs=pl.BlockSpec(memory_space=pl.ANY),
        scratch_shapes=[pltpu.SemaphoreType.DMA],
        compiler_params=pltpu.CompilerParams(vmem_limit_bytes=VMEM_BYTES),
        name="fetch_tiles",
    )(asked, tiles)


def region(slot_of, values, turned, weights, reply):
    points, width_all = values.shape
    width = reply.shape[1]
    chunks = width_all // (2 * width)
    vmem = pl.BlockSpec(memory_space=pltpu.VMEM)
    hbm = pl.BlockSpec(memory_space=pl.ANY)
    return pl.pallas_call(
        region_kernel,
        out_shape=(
            jax.ShapeDtypeStruct(reply.shape, jnp.bfloat16),
            jax.ShapeDtypeStruct((1, points), jnp.float32),
        ),
        in_specs=[pl.BlockSpec(memory_space=pltpu.SMEM), vmem, vmem, vmem, hbm],
        out_specs=(hbm, vmem),
        scratch_shapes=[
            pltpu.VMEM((width_all, width_all), jnp.bfloat16),
            pltpu.VMEM((points, width_all), jnp.bfloat16),
            pltpu.VMEM((width_all, width_all), jnp.bfloat16),
            pltpu.SemaphoreType.DMA((chunks,)),
            pltpu.SemaphoreType.DMA,
        ],
        compiler_params=pltpu.CompilerParams(vmem_limit_bytes=VMEM_BYTES),
        name="region_work",
    )(slot_of, values, turned, weights, reply)


def collect(asked, arrived, stored):
    return pl.pallas_call(
        collect_kernel,
        out_shape=jax.ShapeDtypeStruct((stored,) + arrived.shape[1:], jnp.float32),
        in_specs=[pl.BlockSpec(memory_space=pltpu.SMEM), pl.BlockSpec(memory_space=pl.ANY)],
        out_specs=pl.BlockSpec(memory_space=pltpu.VMEM),
        scratch_shapes=[
            pltpu.VMEM(arrived.shape, jnp.bfloat16),
            pltpu.SemaphoreType.DMA((8,)),
        ],
        compiler_params=pltpu.CompilerParams(vmem_limit_bytes=VMEM_BYTES),
        name="collect_tiles",
    )(asked, arrived)


def per_device(basis_values, grid_weights, density_tiles, tile_index):
    devices = lax.axis_size("row") * lax.axis_size("col")
    stored = density_tiles.shape[0]
    pairs = tile_index.shape[1]
    capacity = 2 * pairs // devices
    slot_total = devices * capacity
    exchange = functools.partial(
        lax.all_to_all, axis_name=AXES, split_axis=0, concat_axis=0, tiled=True
    )
    wanted = tile_index[0]
    owner_of = wanted // stored
    local_of = wanted % stored
    order_ids = jnp.arange(pairs, dtype=jnp.int32)
    earlier = order_ids[:, None] < order_ids[None, :]
    same_owner = owner_of[:, None] == owner_of[None, :]
    position = jnp.sum((same_owner & earlier).astype(jnp.int32), axis=0)
    slot_of = owner_of * capacity + position
    slot_ids = jnp.arange(slot_total, dtype=jnp.int32)
    matches = (slot_of[None, :] == slot_ids[:, None]).astype(jnp.int32)
    send_local = jnp.sum(matches * (local_of + 1)[None, :], axis=1) - 1
    asked = exchange(send_local)
    reply = exchange(fetch(asked, density_tiles))
    values = basis_values[0]
    outgoing, density = region(slot_of, values, values.T, grid_weights, reply)
    arrived = exchange(outgoing)
    return collect(asked, arrived, stored), density


def solution(mesh):
    in_specs = (
        P(AXES, None, None),
        P(AXES, None),
        P(AXES, None, None),
        P(AXES, None),
    )
    out_specs = (P(AXES, None, None), P(AXES, None))
    return jax.shard_map(
        per_device, mesh=mesh, in_specs=in_specs, out_specs=out_specs, check_vma=False
    )
```

```python
import functools

import jax
import jax.numpy as jnp
from jax import lax
from jax.experimental import pallas as pl
from jax.experimental.pallas import tpu as pltpu
from jax.sharding import PartitionSpec as P

exchange_coeff = 0.9847450218426964
AXES = ("row", "col")
VMEM_BYTES = 56 * 1024 * 1024


def fetch_kernel(asked_ref, tiles_ref, out_ref, sem):
    slots = out_ref.shape[0]

    def start(step, carry):
        for lane in range(8):
            slot = step * 8 + lane
            tile = jnp.maximum(asked_ref[slot], 0)
            pltpu.make_async_copy(tiles_ref.at[tile], out_ref.at[slot], sem).start()
        return carry

    lax.fori_loop(0, slots // 8, start, 0)
    pltpu.make_async_copy(out_ref, out_ref, sem).wait()


def region_kernel(
    slot_ref, values_ref, weights_ref, reply_ref, out_ref, density_ref,
    block, scaled, partial, load_sems, store_sem,
):
    points, width_all = values_ref.shape
    width = reply_ref.shape[1]
    sig = width_all // width
    chunk = 4 * width
    chunks = width_all // chunk

    def start_chunk(j):
        for q in range(4 * j, 4 * j + 4):
            for p in range(sig):
                pltpu.make_async_copy(
                    reply_ref.at[slot_ref[p * sig + q]], block.at[q, pl.ds(p * width, width)], load_sems.at[j]
                ).start()

    ahead = 2
    for j in range(ahead):
        start_chunk(j)
    total = jnp.zeros((points, width), jnp.float32)
    for j in range(chunks):
        if j + ahead < chunks:
            start_chunk(j + ahead)
        pair = block.at[pl.ds(4 * j, 4)]
        pltpu.make_async_copy(pair, pair, load_sems.at[j]).wait()
        columns = jnp.concatenate([block[4 * j + k] for k in range(4)], axis=1)
        mixed = jnp.dot(values_ref[...], columns, preferred_element_type=jnp.float32)
        product = mixed * values_ref[:, pl.ds(j * chunk, chunk)].astype(jnp.float32)
        total = total + sum(product[:, k * width:(k + 1) * width] for k in range(4))
    density = jnp.sum(total, axis=1, keepdims=True)
    density = jnp.broadcast_to(density, (points, width))
    density_ref[...] = density.T[:1, :]
    weights = jnp.broadcast_to(weights_ref[...], (width, points)).T
    cube_root = jnp.exp(jnp.log(density * density + 1.0) * (1.0 / 3.0))
    weighted = -exchange_coeff * weights * density / cube_root
    for q in range(sig):
        columns = pl.ds(q * width, width)
        scaled[:, columns] = (weighted * values_ref[:, columns].astype(jnp.float32)).astype(jnp.bfloat16)
    for i in range(chunks):
        rows = pl.ds(i * chunk, chunk)
        result = lax.dot_general(
            values_ref[:, rows], scaled[...], (((0,), (0,)), ((), ())), preferred_element_type=jnp.float32
        ).astype(jnp.bfloat16)
        for half in range(4):
            for q in range(sig):
                pair = (4 * i + half) * sig + q
                partial[pair] = result[half * width:(half + 1) * width, q * width:(q + 1) * width]
                pltpu.make_async_copy(partial.at[pair], out_ref.at[slot_ref[pair]], store_sem).start()
    pltpu.make_async_copy(partial, partial, store_sem).wait()


def collect_kernel(asked_ref, arrived_ref, out_ref, held, sems):
    slots = arrived_ref.shape[0]
    parts = sems.shape[0]
    size = slots // parts

    def piece(j):
        return pltpu.make_async_copy(
            arrived_ref.at[pl.ds(j * size, size)], held.at[pl.ds(j * size, size)], sems.at[j]
        )

    for j in range(parts):
        piece(j).start()
    out_ref[...] = jnp.zeros_like(out_ref)

    def add(slot, carry):
        tile = asked_ref[slot]

        @pl.when(tile >= 0)
        def _():
            out_ref[tile] = out_ref[tile] + held[slot].astype(jnp.float32)

        return carry

    for j in range(parts):
        piece(j).wait()
        lax.fori_loop(j * size, (j + 1) * size, add, 0)


def fetch(asked, tiles):
    slots = asked.shape[0]
    return pl.pallas_call(
        fetch_kernel,
        out_shape=jax.ShapeDtypeStruct((slots,) + tiles.shape[1:], tiles.dtype),
        in_specs=[pl.BlockSpec(memory_space=pltpu.SMEM), pl.BlockSpec(memory_space=pltpu.VMEM)],
        out_specs=pl.BlockSpec(memory_space=pl.ANY),
        scratch_shapes=[pltpu.SemaphoreType.DMA],
        compiler_params=pltpu.CompilerParams(vmem_limit_bytes=VMEM_BYTES),
        name="fetch_tiles",
    )(asked, tiles)


def region(slot_of, values, weights, reply):
    points, width_all = values.shape
    width = reply.shape[1]
    chunks = width_all // (4 * width)
    vmem = pl.BlockSpec(memory_space=pltpu.VMEM)
    hbm = pl.BlockSpec(memory_space=pl.ANY)
    return pl.pallas_call(
        region_kernel,
        out_shape=(
            jax.ShapeDtypeStruct(reply.shape, jnp.bfloat16),
            jax.ShapeDtypeStruct((1, points), jnp.float32),
        ),
        in_specs=[pl.BlockSpec(memory_space=pltpu.SMEM), vmem, vmem, hbm],
        out_specs=(hbm, vmem),
        scratch_shapes=[
            pltpu.VMEM((width_all // width, width_all, width), jnp.bfloat16),
            pltpu.VMEM((points, width_all), jnp.bfloat16),
            pltpu.VMEM((slot_of.shape[0], width, width), jnp.bfloat16),
            pltpu.SemaphoreType.DMA((chunks,)),
            pltpu.SemaphoreType.DMA,
        ],
        compiler_params=pltpu.CompilerParams(vmem_limit_bytes=VMEM_BYTES),
        name="region_work",
    )(slot_of, values, weights, reply)


def collect(asked, arrived, stored):
    return pl.pallas_call(
        collect_kernel,
        out_shape=jax.ShapeDtypeStruct((stored,) + arrived.shape[1:], jnp.float32),
        in_specs=[pl.BlockSpec(memory_space=pltpu.SMEM), pl.BlockSpec(memory_space=pl.ANY)],
        out_specs=pl.BlockSpec(memory_space=pltpu.VMEM),
        scratch_shapes=[
            pltpu.VMEM(arrived.shape, jnp.bfloat16),
            pltpu.SemaphoreType.DMA((8,)),
        ],
        compiler_params=pltpu.CompilerParams(vmem_limit_bytes=VMEM_BYTES),
        name="collect_tiles",
    )(asked, arrived)


def per_device(basis_values, grid_weights, density_tiles, tile_index):
    devices = lax.axis_size("row") * lax.axis_size("col")
    stored = density_tiles.shape[0]
    pairs = tile_index.shape[1]
    capacity = 2 * pairs // devices
    slot_total = devices * capacity
    exchange = functools.partial(
        lax.all_to_all, axis_name=AXES, split_axis=0, concat_axis=0, tiled=True
    )
    wanted = tile_index[0]
    owner_of = wanted // stored
    local_of = wanted % stored
    order_ids = jnp.arange(pairs, dtype=jnp.int32)
    earlier = order_ids[:, None] < order_ids[None, :]
    same_owner = owner_of[:, None] == owner_of[None, :]
    position = jnp.sum((same_owner & earlier).astype(jnp.int32), axis=0)
    slot_of = owner_of * capacity + position
    slot_ids = jnp.arange(slot_total, dtype=jnp.int32)
    matches = (slot_of[None, :] == slot_ids[:, None]).astype(jnp.int32)
    send_local = jnp.sum(matches * (local_of + 1)[None, :], axis=1) - 1
    asked = exchange(send_local)
    reply = exchange(fetch(asked, density_tiles))
    values = basis_values[0]
    outgoing, density = region(slot_of, values, grid_weights, reply)
    arrived = exchange(outgoing)
    return collect(asked, arrived, stored), density


def solution(mesh):
    in_specs = (
        P(AXES, None, None),
        P(AXES, None),
        P(AXES, None, None),
        P(AXES, None),
    )
    out_specs = (P(AXES, None, None), P(AXES, None))
    return jax.shard_map(
        per_device, mesh=mesh, in_specs=in_specs, out_specs=out_specs, check_vma=False
    )
```

```python
import functools

import jax
import jax.numpy as jnp
from jax import lax
from jax.experimental import pallas as pl
from jax.experimental.pallas import tpu as pltpu
from jax.sharding import PartitionSpec as P

exchange_coeff = 0.9847450218426964
AXES = ("row", "col")
VMEM_BYTES = 56 * 1024 * 1024


def fetch_kernel(asked_ref, tiles_ref, out_ref, sem):
    slots = out_ref.shape[0]

    def start(step, carry):
        for lane in range(8):
            slot = step * 8 + lane
            tile = jnp.maximum(asked_ref[slot], 0)
            pltpu.make_async_copy(tiles_ref.at[tile], out_ref.at[slot], sem).start()
        return carry

    lax.fori_loop(0, slots // 8, start, 0)
    pltpu.make_async_copy(out_ref, out_ref, sem).wait()


def region_kernel(
    slot_ref, values_ref, weights_ref, reply_ref, out_ref, density_ref,
    block, scaled, partial, load_sems, store_sem,
):
    points, width_all = values_ref.shape
    width = reply_ref.shape[1]
    sig = width_all // width
    chunk = 4 * width
    chunks = width_all // chunk

    def start_chunk(j):
        for q in range(4 * j, 4 * j + 4):
            for p in range(sig):
                pltpu.make_async_copy(
                    reply_ref.at[slot_ref[p * sig + q]], block.at[q, pl.ds(p * width, width)], load_sems.at[j]
                ).start()

    ahead = 2
    for j in range(ahead):
        start_chunk(j)
    total = jnp.zeros((points, width), jnp.float32)
    for j in range(chunks):
        if j + ahead < chunks:
            start_chunk(j + ahead)
        pair = block.at[pl.ds(4 * j, 4)]
        pltpu.make_async_copy(pair, pair, load_sems.at[j]).wait()
        columns = jnp.concatenate([block[4 * j + k] for k in range(4)], axis=1)
        mixed = jnp.dot(values_ref[...], columns, preferred_element_type=jnp.float32)
        product = mixed * values_ref[:, pl.ds(j * chunk, chunk)].astype(jnp.float32)
        total = total + sum(product[:, k * width:(k + 1) * width] for k in range(4))
    density = jnp.sum(total, axis=1, keepdims=True)
    density = jnp.broadcast_to(density, (points, width))
    density_ref[...] = density.T[:1, :]
    weights = jnp.broadcast_to(weights_ref[...], (width, points)).T
    cube_root = jnp.exp(jnp.log(density * density + 1.0) * (1.0 / 3.0))
    weighted = -exchange_coeff * weights * density / cube_root
    for q in range(sig):
        columns = pl.ds(q * width, width)
        scaled[:, columns] = (weighted * values_ref[:, columns].astype(jnp.float32)).astype(jnp.bfloat16)
    for i in range(chunks):
        rows = pl.ds(i * chunk, chunk)
        result = lax.dot_general(
            values_ref[:, rows], scaled[...], (((0,), (0,)), ((), ())), preferred_element_type=jnp.float32
        ).astype(jnp.bfloat16)
        for half in range(4):
            for q in range(sig):
                pair = (4 * i + half) * sig + q
                partial[pair] = result[half * width:(half + 1) * width, q * width:(q + 1) * width]
                pltpu.make_async_copy(partial.at[pair], out_ref.at[slot_ref[pair]], store_sem).start()
    pltpu.make_async_copy(partial, partial, store_sem).wait()


def collect_kernel(asked_ref, arrived_ref, out_ref, held, sems):
    slots = arrived_ref.shape[0]
    parts = sems.shape[0]
    size = slots // parts

    def piece(j):
        return pltpu.make_async_copy(
            arrived_ref.at[pl.ds(j * size, size)], held.at[pl.ds(j * size, size)], sems.at[j]
        )

    for j in range(parts):
        piece(j).start()
    out_ref[...] = jnp.zeros_like(out_ref)

    def add(slot, carry):
        tile = asked_ref[slot]

        @pl.when(tile >= 0)
        def _():
            out_ref[tile] = out_ref[tile] + held[slot].astype(jnp.float32)

        return carry

    for j in range(parts):
        piece(j).wait()
        lax.fori_loop(j * size, (j + 1) * size, add, 0)


def fetch(asked, tiles):
    slots = asked.shape[0]
    return pl.pallas_call(
        fetch_kernel,
        out_shape=jax.ShapeDtypeStruct((slots,) + tiles.shape[1:], tiles.dtype),
        in_specs=[pl.BlockSpec(memory_space=pltpu.SMEM), pl.BlockSpec(memory_space=pltpu.VMEM)],
        out_specs=pl.BlockSpec(memory_space=pl.ANY),
        scratch_shapes=[pltpu.SemaphoreType.DMA],
        compiler_params=pltpu.CompilerParams(vmem_limit_bytes=VMEM_BYTES),
        name="fetch_tiles",
    )(asked, tiles)


def region(slot_of, values, weights, reply):
    points, width_all = values.shape
    width = reply.shape[1]
    chunks = width_all // (4 * width)
    vmem = pl.BlockSpec(memory_space=pltpu.VMEM)
    hbm = pl.BlockSpec(memory_space=pl.ANY)
    return pl.pallas_call(
        region_kernel,
        out_shape=(
            jax.ShapeDtypeStruct(reply.shape, jnp.bfloat16),
            jax.ShapeDtypeStruct((1, points), jnp.float32),
        ),
        in_specs=[pl.BlockSpec(memory_space=pltpu.SMEM), vmem, vmem, hbm],
        out_specs=(hbm, vmem),
        scratch_shapes=[
            pltpu.VMEM((width_all // width, width_all, width), jnp.bfloat16),
            pltpu.VMEM((points, width_all), jnp.bfloat16),
            pltpu.VMEM((slot_of.shape[0], width, width), jnp.bfloat16),
            pltpu.SemaphoreType.DMA((chunks,)),
            pltpu.SemaphoreType.DMA,
        ],
        compiler_params=pltpu.CompilerParams(vmem_limit_bytes=VMEM_BYTES),
        name="region_work",
    )(slot_of, values, weights, reply)


def collect(asked, arrived, stored):
    return pl.pallas_call(
        collect_kernel,
        out_shape=jax.ShapeDtypeStruct((stored,) + arrived.shape[1:], jnp.float32),
        in_specs=[pl.BlockSpec(memory_space=pltpu.SMEM), pl.BlockSpec(memory_space=pl.ANY)],
        out_specs=pl.BlockSpec(memory_space=pltpu.VMEM),
        scratch_shapes=[
            pltpu.VMEM(arrived.shape, jnp.bfloat16),
            pltpu.SemaphoreType.DMA((8,)),
        ],
        compiler_params=pltpu.CompilerParams(vmem_limit_bytes=VMEM_BYTES),
        name="collect_tiles",
    )(asked, arrived)


def per_device(basis_values, grid_weights, density_tiles, tile_index):
    devices = lax.axis_size("row") * lax.axis_size("col")
    stored = density_tiles.shape[0]
    pairs = tile_index.shape[1]
    capacity = 2 * pairs // devices
    slot_total = devices * capacity
    exchange = functools.partial(
        lax.all_to_all, axis_name=AXES, split_axis=0, concat_axis=0, tiled=True
    )
    wanted = tile_index[0]
    owner_of = wanted // stored
    local_of = wanted % stored
    order_ids = jnp.arange(pairs, dtype=jnp.int32)
    earlier = order_ids[:, None] < order_ids[None, :]
    same_owner = owner_of[:, None] == owner_of[None, :]
    position = jnp.sum((same_owner & earlier).astype(jnp.int32), axis=0)
    slot_of = owner_of * capacity + position
    slot_ids = jnp.arange(slot_total, dtype=jnp.int32)
    matches = (slot_of[None, :] == slot_ids[:, None]).astype(jnp.int32)
    send_local = jnp.sum(matches * (local_of + 1)[None, :], axis=1) - 1
    asked = exchange(send_local)
    fetched = fetch(asked, density_tiles)
    fetched, slot_of, asked = lax.optimization_barrier((fetched, slot_of, asked))
    reply = exchange(fetched)
    values = basis_values[0]
    outgoing, density = region(slot_of, values, grid_weights, reply)
    arrived = exchange(outgoing)
    return collect(asked, arrived, stored), density


def solution(mesh):
    in_specs = (
        P(AXES, None, None),
        P(AXES, None),
        P(AXES, None, None),
        P(AXES, None),
    )
    out_specs = (P(AXES, None, None), P(AXES, None))
    return jax.shard_map(
        per_device, mesh=mesh, in_specs=in_specs, out_specs=out_specs, check_vma=False
    )
```

```python
import functools

import jax
import jax.numpy as jnp
from jax import lax
from jax.experimental import pallas as pl
from jax.experimental.pallas import tpu as pltpu
from jax.sharding import PartitionSpec as P

exchange_coeff = 0.9847450218426964
AXES = ("row", "col")
VMEM_BYTES = 56 * 1024 * 1024
GROUP = 4


def fetch_kernel(asked_ref, tiles_ref, out_ref, sem):
    slots = out_ref.shape[0]

    def start(step, carry):
        for lane in range(8):
            slot = step * 8 + lane
            tile = jnp.maximum(asked_ref[slot], 0)
            pltpu.make_async_copy(tiles_ref.at[tile], out_ref.at[slot], sem).start()
        return carry

    lax.fori_loop(0, slots // 8, start, 0)
    pltpu.make_async_copy(out_ref, out_ref, sem).wait()


def region_kernel(
    slot_ref, values_ref, weights_ref, reply_ref, out_ref, density_ref,
    block, scaled, partial, load_sems, store_sem,
):
    points, width_all = values_ref.shape
    width = reply_ref.shape[1]
    sig = width_all // width
    chunk = 4 * width
    chunks = width_all // chunk

    def start_chunk(j):
        for q in range(4 * j, 4 * j + 4):
            for p in range(sig):
                pltpu.make_async_copy(
                    reply_ref.at[slot_ref[p * sig + q]], block.at[q, pl.ds(p * width, width)], load_sems.at[j]
                ).start()

    ahead = 2
    for j in range(ahead):
        start_chunk(j)
    total = jnp.zeros((points, width), jnp.float32)
    for j in range(chunks):
        if j + ahead < chunks:
            start_chunk(j + ahead)
        pair = block.at[pl.ds(4 * j, 4)]
        pltpu.make_async_copy(pair, pair, load_sems.at[j]).wait()
        columns = jnp.concatenate([block[4 * j + k] for k in range(4)], axis=1)
        mixed = jnp.dot(values_ref[...], columns, preferred_element_type=jnp.float32)
        product = mixed * values_ref[:, pl.ds(j * chunk, chunk)].astype(jnp.float32)
        total = total + sum(product[:, k * width:(k + 1) * width] for k in range(4))
    density = jnp.sum(total, axis=1, keepdims=True)
    density = jnp.broadcast_to(density, (points, width))
    density_ref[...] = density.T[:1, :]
    weights = jnp.broadcast_to(weights_ref[...], (width, points)).T
    cube_root = jnp.exp(jnp.log(density * density + 1.0) * (1.0 / 3.0))
    weighted = -exchange_coeff * weights * density / cube_root
    for q in range(sig):
        columns = pl.ds(q * width, width)
        scaled[:, columns] = (weighted * values_ref[:, columns].astype(jnp.float32)).astype(jnp.bfloat16)
    for i in range(chunks):
        rows = pl.ds(i * chunk, chunk)
        result = lax.dot_general(
            values_ref[:, rows], scaled[...], (((0,), (0,)), ((), ())), preferred_element_type=jnp.float32
        ).astype(jnp.bfloat16)
        for half in range(4):
            for q in range(sig):
                pair = (4 * i + half) * sig + q
                partial[pair] = result[half * width:(half + 1) * width, q * width:(q + 1) * width]
                pltpu.make_async_copy(partial.at[pair], out_ref.at[slot_ref[pair]], store_sem).start()
    pltpu.make_async_copy(partial, partial, store_sem).wait()


def collect_kernel(asked_ref, arrived_ref, out_ref, held, spare, seen, sems):
    slots = arrived_ref.shape[0]
    stored = out_ref.shape[0]
    parts = sems.shape[0]
    size = slots // parts

    def piece(j):
        return pltpu.make_async_copy(
            arrived_ref.at[pl.ds(j * size, size)], held.at[pl.ds(j * size, size)], sems.at[j]
        )

    for j in range(parts):
        piece(j).start()

    def forget(tile, carry):
        seen[tile] = 0
        return carry

    lax.fori_loop(0, stored + 1, forget, 0)

    def add(group, carry):
        base = group * GROUP
        tiles = [asked_ref[base + k] for k in range(GROUP)]
        tiles = [jnp.where(tile < 0, stored, tile) for tile in tiles]
        kept = [seen[tile] > 0 for tile in tiles]
        sums = []
        for k in range(GROUP):
            before = spare[tiles[k]]
            sums.append(jnp.where(kept[k], before, 0.0) + held[base + k].astype(jnp.float32))
        for k in range(GROUP):
            spare[tiles[k]] = sums[k]
            seen[tiles[k]] = 1
        return carry

    for j in range(parts):
        piece(j).wait()
        lax.fori_loop(j * size // GROUP, (j + 1) * size // GROUP, add, 0)

    def clear(tile, carry):
        @pl.when(seen[tile] == 0)
        def _():
            spare[tile] = jnp.zeros(spare.shape[1:], jnp.float32)

        return carry

    lax.fori_loop(0, stored, clear, 0)
    total = spare.at[pl.ds(0, stored)]
    done = pltpu.make_async_copy(total, out_ref, sems.at[0])
    done.start()
    done.wait()


def fetch(asked, tiles):
    slots = asked.shape[0]
    return pl.pallas_call(
        fetch_kernel,
        out_shape=jax.ShapeDtypeStruct((slots,) + tiles.shape[1:], tiles.dtype),
        in_specs=[pl.BlockSpec(memory_space=pltpu.SMEM), pl.BlockSpec(memory_space=pltpu.VMEM)],
        out_specs=pl.BlockSpec(memory_space=pl.ANY),
        scratch_shapes=[pltpu.SemaphoreType.DMA],
        compiler_params=pltpu.CompilerParams(vmem_limit_bytes=VMEM_BYTES),
        name="fetch_tiles",
    )(asked, tiles)


def region(slot_of, values, weights, reply):
    points, width_all = values.shape
    width = reply.shape[1]
    chunks = width_all // (4 * width)
    vmem = pl.BlockSpec(memory_space=pltpu.VMEM)
    hbm = pl.BlockSpec(memory_space=pl.ANY)
    return pl.pallas_call(
        region_kernel,
        out_shape=(
            jax.ShapeDtypeStruct(reply.shape, jnp.bfloat16),
            jax.ShapeDtypeStruct((1, points), jnp.float32),
        ),
        in_specs=[pl.BlockSpec(memory_space=pltpu.SMEM), vmem, vmem, hbm],
        out_specs=(hbm, vmem),
        scratch_shapes=[
            pltpu.VMEM((width_all // width, width_all, width), jnp.bfloat16),
            pltpu.VMEM((points, width_all), jnp.bfloat16),
            pltpu.VMEM((slot_of.shape[0], width, width), jnp.bfloat16),
            pltpu.SemaphoreType.DMA((chunks,)),
            pltpu.SemaphoreType.DMA,
        ],
        compiler_params=pltpu.CompilerParams(vmem_limit_bytes=VMEM_BYTES),
        name="region_work",
    )(slot_of, values, weights, reply)


def collect(asked, arrived, stored):
    return pl.pallas_call(
        collect_kernel,
        out_shape=jax.ShapeDtypeStruct((stored,) + arrived.shape[1:], jnp.float32),
        in_specs=[pl.BlockSpec(memory_space=pltpu.SMEM), pl.BlockSpec(memory_space=pl.ANY)],
        out_specs=pl.BlockSpec(memory_space=pl.ANY),
        scratch_shapes=[
            pltpu.VMEM(arrived.shape, jnp.bfloat16),
            pltpu.VMEM((stored + 1,) + arrived.shape[1:], jnp.float32),
            pltpu.SMEM((stored + 1,), jnp.int32),
            pltpu.SemaphoreType.DMA((8,)),
        ],
        compiler_params=pltpu.CompilerParams(vmem_limit_bytes=VMEM_BYTES),
        name="collect_tiles",
    )(asked, arrived)


def per_device(basis_values, grid_weights, density_tiles, tile_index):
    devices = lax.axis_size("row") * lax.axis_size("col")
    stored = density_tiles.shape[0]
    pairs = tile_index.shape[1]
    capacity = 2 * pairs // devices
    slot_total = devices * capacity
    exchange = functools.partial(
        lax.all_to_all, axis_name=AXES, split_axis=0, concat_axis=0, tiled=True
    )
    wanted = tile_index[0]
    owner_of = wanted // stored
    local_of = wanted % stored
    order_ids = jnp.arange(pairs, dtype=jnp.int32)
    earlier = order_ids[:, None] < order_ids[None, :]
    same_owner = owner_of[:, None] == owner_of[None, :]
    position = jnp.sum((same_owner & earlier).astype(jnp.int32), axis=0)
    slot_of = owner_of * capacity + position
    slot_ids = jnp.arange(slot_total, dtype=jnp.int32)
    matches = (slot_of[None, :] == slot_ids[:, None]).astype(jnp.int32)
    send_local = jnp.sum(matches * (local_of + 1)[None, :], axis=1) - 1
    tiles = pltpu.with_memory_space_constraint(density_tiles, pltpu.VMEM)
    send_local, tiles = lax.optimization_barrier((send_local, tiles))
    asked = exchange(send_local)
    fetched = fetch(asked, tiles)
    fetched, slot_of, asked = lax.optimization_barrier((fetched, slot_of, asked))
    reply = exchange(fetched)
    values = pltpu.with_memory_space_constraint(basis_values[0], pltpu.VMEM)
    outgoing, density = region(slot_of, values, grid_weights, reply)
    arrived = exchange(outgoing)
    return collect(asked, arrived, stored), density


def solution(mesh):
    in_specs = (
        P(AXES, None, None),
        P(AXES, None),
        P(AXES, None, None),
        P(AXES, None),
    )
    out_specs = (P(AXES, None, None), P(AXES, None))
    return jax.shard_map(
        per_device, mesh=mesh, in_specs=in_specs, out_specs=out_specs, check_vma=False
    )
```

```python
import functools

import jax
import jax.numpy as jnp
from jax import lax
from jax.experimental import pallas as pl
from jax.experimental.pallas import tpu as pltpu
from jax.sharding import PartitionSpec as P

exchange_coeff = 0.9847450218426964
AXES = ("row", "col")
VMEM_BYTES = 56 * 1024 * 1024
GROUP = 4
PARTS = 2


def fetch_kernel(asked_ref, tiles_ref, out_ref, sem):
    slots = out_ref.shape[0]

    def start(step, carry):
        for lane in range(8):
            slot = step * 8 + lane
            tile = jnp.maximum(asked_ref[slot], 0)
            pltpu.make_async_copy(tiles_ref.at[tile], out_ref.at[slot], sem).start()
        return carry

    lax.fori_loop(0, slots // 8, start, 0)
    pltpu.make_async_copy(out_ref, out_ref, sem).wait()


def region_kernel(
    slot_ref, values_ref, weights_ref, reply_ref, out_ref, density_ref,
    block, scaled, partial, store_sem,
):
    points, width_all = values_ref.shape
    width = reply_ref.shape[1]
    sig = width_all // width
    chunk = 4 * width
    chunks = width_all // chunk

    total = jnp.zeros((points, width), jnp.float32)
    for j in range(chunks):
        for q in range(4 * j, 4 * j + 4):
            for p in range(sig):
                block[q, pl.ds(p * width, width)] = reply_ref[slot_ref[p * sig + q]]
        columns = jnp.concatenate([block[4 * j + k] for k in range(4)], axis=1)
        mixed = jnp.dot(values_ref[...], columns, preferred_element_type=jnp.float32)
        product = mixed * values_ref[:, pl.ds(j * chunk, chunk)].astype(jnp.float32)
        total = total + sum(product[:, k * width:(k + 1) * width] for k in range(4))
    density = jnp.sum(total, axis=1, keepdims=True)
    density = jnp.broadcast_to(density, (points, width))
    density_ref[...] = density.T[:1, :]
    weights = jnp.broadcast_to(weights_ref[...], (width, points)).T
    cube_root = jnp.exp(jnp.log(density * density + 1.0) * (1.0 / 3.0))
    weighted = -exchange_coeff * weights * density / cube_root
    for q in range(sig):
        columns = pl.ds(q * width, width)
        scaled[:, columns] = (weighted * values_ref[:, columns].astype(jnp.float32)).astype(jnp.bfloat16)
    for i in range(chunks):
        rows = pl.ds(i * chunk, chunk)
        result = lax.dot_general(
            values_ref[:, rows], scaled[...], (((0,), (0,)), ((), ())), preferred_element_type=jnp.float32
        ).astype(jnp.bfloat16)
        for half in range(4):
            for q in range(sig):
                pair = (4 * i + half) * sig + q
                partial[pair] = result[half * width:(half + 1) * width, q * width:(q + 1) * width]
                pltpu.make_async_copy(partial.at[pair], out_ref.at[slot_ref[pair]], store_sem).start()
    pltpu.make_async_copy(partial, partial, store_sem).wait()


def collect_kernel(asked_ref, arrived_ref, out_ref, held, seen, sems):
    slots = arrived_ref.shape[0]
    stored, width = out_ref.shape[:2]
    parts = sems.shape[0]
    height = width // parts

    def forget(tile, carry):
        seen[tile] = 0
        return carry

    lax.fori_loop(0, stored + 1, forget, 0, unroll=8)

    def strip(part):
        rows = pl.ds(part * height, height)
        return pltpu.make_async_copy(held.at[pl.ds(0, stored), rows], out_ref.at[:, rows], sems.at[part])

    def clear(tile, carry):
        @pl.when(seen[tile] == 0)
        def _():
            held[tile] = jnp.zeros(held.shape[1:], jnp.float32)

        return carry

    for part in range(parts):
        rows = pl.ds(part * height, height)

        def add(group, carry):
            base = group * GROUP
            tiles = [asked_ref[base + k] for k in range(GROUP)]
            tiles = [jnp.where(tile < 0, stored, tile) for tile in tiles]
            kept = [seen[tile] > part for tile in tiles]
            sums = []
            for k in range(GROUP):
                before = held[tiles[k], rows]
                sums.append(jnp.where(kept[k], before, 0.0) + arrived_ref[base + k, rows].astype(jnp.float32))
            for k in range(GROUP):
                held[tiles[k], rows] = sums[k]
                seen[tiles[k]] = part + 1
            return carry

        lax.fori_loop(0, slots // GROUP, add, 0)
        if part == 0:
            lax.fori_loop(0, stored, clear, 0)
        strip(part).start()
    for part in range(parts):
        strip(part).wait()


def fetch(asked, tiles):
    slots = asked.shape[0]
    return pl.pallas_call(
        fetch_kernel,
        out_shape=jax.ShapeDtypeStruct((slots,) + tiles.shape[1:], tiles.dtype),
        in_specs=[pl.BlockSpec(memory_space=pltpu.SMEM), pl.BlockSpec(memory_space=pltpu.VMEM)],
        out_specs=pl.BlockSpec(memory_space=pl.ANY),
        scratch_shapes=[pltpu.SemaphoreType.DMA],
        compiler_params=pltpu.CompilerParams(vmem_limit_bytes=VMEM_BYTES),
        name="fetch_tiles",
    )(asked, tiles)


def region(slot_of, values, weights, reply):
    points, width_all = values.shape
    width = reply.shape[1]
    vmem = pl.BlockSpec(memory_space=pltpu.VMEM)
    hbm = pl.BlockSpec(memory_space=pl.ANY)
    return pl.pallas_call(
        region_kernel,
        out_shape=(
            jax.ShapeDtypeStruct(reply.shape, jnp.bfloat16),
            jax.ShapeDtypeStruct((1, points), jnp.float32),
        ),
        in_specs=[pl.BlockSpec(memory_space=pltpu.SMEM), vmem, vmem, vmem],
        out_specs=(hbm, vmem),
        scratch_shapes=[
            pltpu.VMEM((width_all // width, width_all, width), jnp.bfloat16),
            pltpu.VMEM((points, width_all), jnp.bfloat16),
            pltpu.VMEM((slot_of.shape[0], width, width), jnp.bfloat16),
            pltpu.SemaphoreType.DMA,
        ],
        compiler_params=pltpu.CompilerParams(vmem_limit_bytes=34 * 1024 * 1024),
        name="region_work",
    )(slot_of, values, weights, reply)


def collect(asked, arrived, stored):
    return pl.pallas_call(
        collect_kernel,
        out_shape=jax.ShapeDtypeStruct((stored,) + arrived.shape[1:], jnp.float32),
        in_specs=[pl.BlockSpec(memory_space=pltpu.SMEM), pl.BlockSpec(memory_space=pltpu.VMEM)],
        out_specs=pl.BlockSpec(memory_space=pl.ANY),
        scratch_shapes=[
            pltpu.VMEM((stored + 1,) + arrived.shape[1:], jnp.float32),
            pltpu.SMEM((stored + 1,), jnp.int32),
            pltpu.SemaphoreType.DMA((PARTS,)),
        ],
        compiler_params=pltpu.CompilerParams(vmem_limit_bytes=20 * 1024 * 1024),
        name="collect_tiles",
    )(asked, arrived)


def per_device(basis_values, grid_weights, density_tiles, tile_index):
    devices = lax.axis_size("row") * lax.axis_size("col")
    stored = density_tiles.shape[0]
    pairs = tile_index.shape[1]
    capacity = 2 * pairs // devices
    slot_total = devices * capacity
    exchange = functools.partial(
        lax.all_to_all, axis_name=AXES, split_axis=0, concat_axis=0, tiled=True
    )
    wanted = tile_index[0]
    owner_of = wanted // stored
    local_of = wanted % stored
    order_ids = jnp.arange(pairs, dtype=jnp.int32)
    earlier = order_ids[:, None] < order_ids[None, :]
    same_owner = owner_of[:, None] == owner_of[None, :]
    position = jnp.sum((same_owner & earlier).astype(jnp.int32), axis=0)
    slot_of = owner_of * capacity + position
    slot_ids = jnp.arange(slot_total, dtype=jnp.int32)
    matches = (slot_of[None, :] == slot_ids[:, None]).astype(jnp.int32)
    send_local = jnp.sum(matches * (local_of + 1)[None, :], axis=1) - 1
    asked = exchange(send_local)
    fetched = fetch(asked, density_tiles)
    fetched, slot_of, asked = lax.optimization_barrier((fetched, slot_of, asked))
    reply = pltpu.with_memory_space_constraint(exchange(fetched), pltpu.VMEM)
    values = pltpu.with_memory_space_constraint(basis_values[0], pltpu.VMEM)
    outgoing, density = region(slot_of, values, grid_weights, reply)
    arrived = pltpu.with_memory_space_constraint(exchange(outgoing), pltpu.VMEM)
    return collect(asked, arrived, stored), density


def solution(mesh):
    in_specs = (
        P(AXES, None, None),
        P(AXES, None),
        P(AXES, None, None),
        P(AXES, None),
    )
    out_specs = (P(AXES, None, None), P(AXES, None))
    return jax.shard_map(
        per_device, mesh=mesh, in_specs=in_specs, out_specs=out_specs, check_vma=False
    )
```

```python
import functools

import jax
import jax.numpy as jnp
from jax import lax
from jax.experimental import pallas as pl
from jax.experimental.pallas import tpu as pltpu
from jax.sharding import PartitionSpec as P

exchange_coeff = 0.9847450218426964
AXES = ("row", "col")
VMEM_BYTES = 56 * 1024 * 1024
GROUP = 4
PARTS = 2


def fetch_kernel(asked_ref, tiles_ref, out_ref, sem):
    slots = out_ref.shape[0]

    def start(step, carry):
        for lane in range(8):
            slot = step * 8 + lane
            tile = jnp.maximum(asked_ref[step * (8 // GROUP) + lane // GROUP, lane % GROUP], 0)
            pltpu.make_async_copy(tiles_ref.at[tile], out_ref.at[slot], sem).start()
        return carry

    lax.fori_loop(0, slots // 8, start, 0)
    pltpu.make_async_copy(out_ref, out_ref, sem).wait()


def region_kernel(
    slot_ref, values_ref, weights_ref, reply_ref, out_ref, density_ref,
    block, scaled, partial, store_sem,
):
    points, width_all = values_ref.shape
    width = reply_ref.shape[1]
    sig = width_all // width
    chunk = 4 * width
    chunks = width_all // chunk

    total = jnp.zeros((points, width), jnp.float32)
    for j in range(chunks):
        for q in range(4 * j, 4 * j + 4):
            for p in range(sig):
                block[q, pl.ds(p * width, width)] = reply_ref[slot_ref[p * sig + q]]
        columns = jnp.concatenate([block[4 * j + k] for k in range(4)], axis=1)
        mixed = jnp.dot(values_ref[...], columns, preferred_element_type=jnp.float32)
        product = mixed * values_ref[:, pl.ds(j * chunk, chunk)].astype(jnp.float32)
        total = total + sum(product[:, k * width:(k + 1) * width] for k in range(4))
    density = jnp.sum(total, axis=1, keepdims=True)
    density = jnp.broadcast_to(density, (points, width))
    density_ref[...] = density.T[:1, :]
    weights = jnp.broadcast_to(weights_ref[...], (width, points)).T
    cube_root = jnp.exp(jnp.log(density * density + 1.0) * (1.0 / 3.0))
    weighted = -exchange_coeff * weights * density / cube_root
    for q in range(sig):
        columns = pl.ds(q * width, width)
        scaled[:, columns] = (weighted * values_ref[:, columns].astype(jnp.float32)).astype(jnp.bfloat16)
    for i in range(chunks):
        rows = pl.ds(i * chunk, chunk)
        result = lax.dot_general(
            values_ref[:, rows], scaled[...], (((0,), (0,)), ((), ())), preferred_element_type=jnp.float32
        ).astype(jnp.bfloat16)
        for half in range(4):
            for q in range(sig):
                pair = (4 * i + half) * sig + q
                partial[pair] = result[half * width:(half + 1) * width, q * width:(q + 1) * width]
                pltpu.make_async_copy(partial.at[pair], out_ref.at[slot_ref[pair]], store_sem).start()
    pltpu.make_async_copy(partial, partial, store_sem).wait()


def collect_kernel(asked_ref, arrived_ref, out_ref, held, seen, sems):
    slots = arrived_ref.shape[0]
    stored, width = out_ref.shape[:2]
    parts = sems.shape[0]
    height = width // parts

    def forget(tile, carry):
        seen[tile] = 0
        return carry

    lax.fori_loop(0, stored + 1, forget, 0, unroll=8)

    def strip(part):
        rows = pl.ds(part * height, height)
        return pltpu.make_async_copy(held.at[pl.ds(0, stored), rows], out_ref.at[:, rows], sems.at[part])

    def clear(tile, carry):
        @pl.when(seen[tile] == 0)
        def _():
            held[tile] = jnp.zeros(held.shape[1:], jnp.float32)

        return carry

    for part in range(parts):
        rows = pl.ds(part * height, height)

        def add(group, carry):
            base = group * GROUP
            tiles = [asked_ref[group, k] for k in range(GROUP)]
            tiles = [jnp.where(tile < 0, stored, tile) for tile in tiles]
            kept = [seen[tile] > part for tile in tiles]
            sums = []
            for k in range(GROUP):
                before = held[tiles[k], rows]
                sums.append(jnp.where(kept[k], before, 0.0) + arrived_ref[base + k, rows].astype(jnp.float32))
            for k in range(GROUP):
                held[tiles[k], rows] = sums[k]
                seen[tiles[k]] = part + 1
            return carry

        lax.fori_loop(0, slots // GROUP, add, 0)
        if part == 0:
            lax.fori_loop(0, stored, clear, 0)
        strip(part).start()
    for part in range(parts):
        strip(part).wait()


def fetch(asked, tiles):
    slots = asked.shape[0] * GROUP
    return pl.pallas_call(
        fetch_kernel,
        out_shape=jax.ShapeDtypeStruct((slots,) + tiles.shape[1:], tiles.dtype),
        in_specs=[pl.BlockSpec(memory_space=pltpu.SMEM), pl.BlockSpec(memory_space=pltpu.VMEM)],
        out_specs=pl.BlockSpec(memory_space=pl.ANY),
        scratch_shapes=[pltpu.SemaphoreType.DMA],
        compiler_params=pltpu.CompilerParams(vmem_limit_bytes=VMEM_BYTES),
        name="fetch_tiles",
    )(asked, tiles)


def region(slot_of, values, weights, reply):
    points, width_all = values.shape
    width = reply.shape[1]
    vmem = pl.BlockSpec(memory_space=pltpu.VMEM)
    hbm = pl.BlockSpec(memory_space=pl.ANY)
    return pl.pallas_call(
        region_kernel,
        out_shape=(
            jax.ShapeDtypeStruct(reply.shape, jnp.bfloat16),
            jax.ShapeDtypeStruct((1, points), jnp.float32),
        ),
        in_specs=[pl.BlockSpec(memory_space=pltpu.SMEM), vmem, vmem, vmem],
        out_specs=(hbm, vmem),
        scratch_shapes=[
            pltpu.VMEM((width_all // width, width_all, width), jnp.bfloat16),
            pltpu.VMEM((points, width_all), jnp.bfloat16),
            pltpu.VMEM((slot_of.shape[0], width, width), jnp.bfloat16),
            pltpu.SemaphoreType.DMA,
        ],
        compiler_params=pltpu.CompilerParams(vmem_limit_bytes=34 * 1024 * 1024),
        name="region_work",
    )(slot_of, values, weights, reply)


def collect(asked, arrived, stored):
    return pl.pallas_call(
        collect_kernel,
        out_shape=jax.ShapeDtypeStruct((stored,) + arrived.shape[1:], jnp.float32),
        in_specs=[pl.BlockSpec(memory_space=pltpu.SMEM), pl.BlockSpec(memory_space=pltpu.VMEM)],
        out_specs=pl.BlockSpec(memory_space=pl.ANY),
        scratch_shapes=[
            pltpu.VMEM((stored + 1,) + arrived.shape[1:], jnp.float32),
            pltpu.SMEM((stored + 1,), jnp.int32),
            pltpu.SemaphoreType.DMA((PARTS,)),
        ],
        compiler_params=pltpu.CompilerParams(vmem_limit_bytes=20 * 1024 * 1024),
        name="collect_tiles",
    )(asked, arrived)


def per_device(basis_values, grid_weights, density_tiles, tile_index):
    devices = lax.axis_size("row") * lax.axis_size("col")
    stored = density_tiles.shape[0]
    pairs = tile_index.shape[1]
    capacity = 2 * pairs // devices
    exchange = functools.partial(
        lax.all_to_all, axis_name=AXES, split_axis=0, concat_axis=0, tiled=True
    )
    wanted = tile_index[0]
    owner_of = wanted // stored
    local_of = wanted % stored
    order_ids = jnp.arange(pairs, dtype=jnp.int32)
    earlier = order_ids[:, None] < order_ids[None, :]
    same_owner = owner_of[:, None] == owner_of[None, :]
    position = jnp.sum((same_owner & earlier).astype(jnp.int32), axis=0)
    slot_of = owner_of * capacity + position
    device_ids = jnp.arange(devices, dtype=jnp.int32)
    lanes = jnp.arange(stored, dtype=jnp.int32)
    to_owner = (owner_of[None, :] == device_ids[:, None]).astype(jnp.bfloat16)
    named = jnp.where(position[:, None] == lanes[None, :], (local_of + 1)[:, None], 0)
    send_local = jnp.dot(to_owner, named.astype(jnp.bfloat16), preferred_element_type=jnp.float32)
    asked = exchange(send_local.astype(jnp.int32) - 1)
    fetched = fetch(asked, density_tiles)
    fetched, slot_of, asked = lax.optimization_barrier((fetched, slot_of, asked))
    reply = pltpu.with_memory_space_constraint(exchange(fetched), pltpu.VMEM)
    values = pltpu.with_memory_space_constraint(basis_values[0], pltpu.VMEM)
    outgoing, density = region(slot_of, values, grid_weights, reply)
    arrived = pltpu.with_memory_space_constraint(exchange(outgoing), pltpu.VMEM)
    return collect(asked, arrived, stored), density


def solution(mesh):
    in_specs = (
        P(AXES, None, None),
        P(AXES, None),
        P(AXES, None, None),
        P(AXES, None),
    )
    out_specs = (P(AXES, None, None), P(AXES, None))
    return jax.shard_map(
        per_device, mesh=mesh, in_specs=in_specs, out_specs=out_specs, check_vma=False
    )
```

```python
import functools

import jax
import jax.numpy as jnp
from jax import lax
from jax.experimental import pallas as pl
from jax.experimental.pallas import tpu as pltpu
from jax.sharding import PartitionSpec as P

exchange_coeff = 0.9847450218426964
AXES = ("row", "col")
VMEM_BYTES = 56 * 1024 * 1024
GROUP = 4
PARTS = 2


def fetch_kernel(asked_ref, tiles_ref, out_ref, flat_ref, sem):
    slots = out_ref.shape[0]

    def start(step, carry):
        for lane in range(8):
            slot = step * 8 + lane
            named = asked_ref[step * (8 // GROUP) + lane // GROUP, lane % GROUP]
            flat_ref[slot] = named
            tile = jnp.maximum(named, 0)
            pltpu.make_async_copy(tiles_ref.at[tile], out_ref.at[slot], sem).start()
        return carry

    lax.fori_loop(0, slots // 8, start, 0)
    pltpu.make_async_copy(out_ref, out_ref, sem).wait()


def region_kernel(
    slot_ref, values_ref, weights_ref, reply_ref, out_ref, density_ref,
    block, scaled, partial, store_sem,
):
    points, width_all = values_ref.shape
    width = reply_ref.shape[1]
    sig = width_all // width
    chunk = 4 * width
    chunks = width_all // chunk

    total = jnp.zeros((points, width), jnp.float32)
    for j in range(chunks):
        for q in range(4 * j, 4 * j + 4):
            for p in range(sig):
                block[q, pl.ds(p * width, width)] = reply_ref[slot_ref[p * sig + q]]
        columns = jnp.concatenate([block[4 * j + k] for k in range(4)], axis=1)
        mixed = jnp.dot(values_ref[...], columns, preferred_element_type=jnp.float32)
        product = mixed * values_ref[:, pl.ds(j * chunk, chunk)].astype(jnp.float32)
        total = total + sum(product[:, k * width:(k + 1) * width] for k in range(4))
    density = jnp.sum(total, axis=1, keepdims=True)
    density = jnp.broadcast_to(density, (points, width))
    density_ref[...] = density.T[:1, :]
    weights = jnp.broadcast_to(weights_ref[...], (width, points)).T
    cube_root = jnp.exp(jnp.log(density * density + 1.0) * (1.0 / 3.0))
    weighted = -exchange_coeff * weights * density / cube_root
    for q in range(sig):
        columns = pl.ds(q * width, width)
        scaled[:, columns] = (weighted * values_ref[:, columns].astype(jnp.float32)).astype(jnp.bfloat16)
    for i in range(chunks):
        rows = pl.ds(i * chunk, chunk)
        result = lax.dot_general(
            values_ref[:, rows], scaled[...], (((0,), (0,)), ((), ())), preferred_element_type=jnp.float32
        ).astype(jnp.bfloat16)
        for half in range(4):
            for q in range(sig):
                pair = (4 * i + half) * sig + q
                partial[pair] = result[half * width:(half + 1) * width, q * width:(q + 1) * width]
                pltpu.make_async_copy(partial.at[pair], out_ref.at[slot_ref[pair]], store_sem).start()
    pltpu.make_async_copy(partial, partial, store_sem).wait()


def collect_kernel(asked_ref, arrived_ref, out_ref, held, seen, sems):
    slots = arrived_ref.shape[0]
    stored, width = out_ref.shape[:2]
    parts = sems.shape[0]
    height = width // parts

    def forget(tile, carry):
        seen[tile] = 0
        return carry

    lax.fori_loop(0, stored + 1, forget, 0, unroll=8)

    def strip(part):
        rows = pl.ds(part * height, height)
        return pltpu.make_async_copy(held.at[pl.ds(0, stored), rows], out_ref.at[:, rows], sems.at[part])

    def clear(tile, carry):
        @pl.when(seen[tile] == 0)
        def _():
            held[tile] = jnp.zeros(held.shape[1:], jnp.float32)

        return carry

    for part in range(parts):
        rows = pl.ds(part * height, height)

        def add(group, carry):
            base = group * GROUP
            tiles = [asked_ref[base + k] for k in range(GROUP)]
            tiles = [jnp.where(tile < 0, stored, tile) for tile in tiles]
            kept = [seen[tile] > part for tile in tiles]
            sums = []
            for k in range(GROUP):
                before = held[tiles[k], rows]
                sums.append(jnp.where(kept[k], before, 0.0) + arrived_ref[base + k, rows].astype(jnp.float32))
            for k in range(GROUP):
                held[tiles[k], rows] = sums[k]
                seen[tiles[k]] = part + 1
            return carry

        lax.fori_loop(0, slots // GROUP, add, 0)
        if part == 0:
            lax.fori_loop(0, stored, clear, 0)
        strip(part).start()
    for part in range(parts):
        strip(part).wait()


def fetch(asked, tiles):
    slots = asked.shape[0] * GROUP
    return pl.pallas_call(
        fetch_kernel,
        out_shape=(
            jax.ShapeDtypeStruct((slots,) + tiles.shape[1:], tiles.dtype),
            jax.ShapeDtypeStruct((slots,), jnp.int32),
        ),
        in_specs=[pl.BlockSpec(memory_space=pltpu.SMEM), pl.BlockSpec(memory_space=pltpu.VMEM)],
        out_specs=(pl.BlockSpec(memory_space=pl.ANY), pl.BlockSpec(memory_space=pltpu.SMEM)),
        scratch_shapes=[pltpu.SemaphoreType.DMA],
        compiler_params=pltpu.CompilerParams(vmem_limit_bytes=VMEM_BYTES),
        name="fetch_tiles",
    )(asked, tiles)


def region(slot_of, values, weights, reply):
    points, width_all = values.shape
    width = reply.shape[1]
    vmem = pl.BlockSpec(memory_space=pltpu.VMEM)
    hbm = pl.BlockSpec(memory_space=pl.ANY)
    return pl.pallas_call(
        region_kernel,
        out_shape=(
            jax.ShapeDtypeStruct(reply.shape, jnp.bfloat16),
            jax.ShapeDtypeStruct((1, points), jnp.float32),
        ),
        in_specs=[pl.BlockSpec(memory_space=pltpu.SMEM), vmem, vmem, vmem],
        out_specs=(hbm, vmem),
        scratch_shapes=[
            pltpu.VMEM((width_all // width, width_all, width), jnp.bfloat16),
            pltpu.VMEM((points, width_all), jnp.bfloat16),
            pltpu.VMEM((slot_of.shape[0], width, width), jnp.bfloat16),
            pltpu.SemaphoreType.DMA,
        ],
        compiler_params=pltpu.CompilerParams(vmem_limit_bytes=34 * 1024 * 1024),
        name="region_work",
    )(slot_of, values, weights, reply)


def collect(asked, arrived, stored):
    return pl.pallas_call(
        collect_kernel,
        out_shape=jax.ShapeDtypeStruct((stored,) + arrived.shape[1:], jnp.float32),
        in_specs=[pl.BlockSpec(memory_space=pltpu.SMEM), pl.BlockSpec(memory_space=pltpu.VMEM)],
        out_specs=pl.BlockSpec(memory_space=pl.ANY),
        scratch_shapes=[
            pltpu.VMEM((stored + 1,) + arrived.shape[1:], jnp.float32),
            pltpu.SMEM((stored + 1,), jnp.int32),
            pltpu.SemaphoreType.DMA((PARTS,)),
        ],
        compiler_params=pltpu.CompilerParams(vmem_limit_bytes=20 * 1024 * 1024),
        name="collect_tiles",
    )(asked, arrived)


def per_device(basis_values, grid_weights, density_tiles, tile_index):
    devices = lax.axis_size("row") * lax.axis_size("col")
    stored = density_tiles.shape[0]
    pairs = tile_index.shape[1]
    capacity = 2 * pairs // devices
    exchange = functools.partial(
        lax.all_to_all, axis_name=AXES, split_axis=0, concat_axis=0, tiled=True
    )
    wanted = tile_index[0]
    owner_of = wanted // stored
    local_of = wanted % stored
    order_ids = jnp.arange(pairs, dtype=jnp.int32)
    earlier = order_ids[:, None] < order_ids[None, :]
    same_owner = owner_of[:, None] == owner_of[None, :]
    position = jnp.sum((same_owner & earlier).astype(jnp.int32), axis=0)
    slot_of = owner_of * capacity + position
    device_ids = jnp.arange(devices, dtype=jnp.int32)
    lanes = jnp.arange(stored, dtype=jnp.int32)
    to_owner = (owner_of[None, :] == device_ids[:, None]).astype(jnp.bfloat16)
    named = jnp.where(position[:, None] == lanes[None, :], (local_of + 1)[:, None], 0)
    send_local = jnp.dot(to_owner, named.astype(jnp.bfloat16), preferred_element_type=jnp.float32)
    asked = exchange(send_local.astype(jnp.int32) - 1)
    fetched, asked = fetch(asked, density_tiles)
    fetched, slot_of, asked = lax.optimization_barrier((fetched, slot_of, asked))
    reply = pltpu.with_memory_space_constraint(exchange(fetched), pltpu.VMEM)
    values = pltpu.with_memory_space_constraint(basis_values[0], pltpu.VMEM)
    outgoing, density = region(slot_of, values, grid_weights, reply)
    arrived = pltpu.with_memory_space_constraint(exchange(outgoing), pltpu.VMEM)
    return collect(asked, arrived, stored), density


def solution(mesh):
    in_specs = (
        P(AXES, None, None),
        P(AXES, None),
        P(AXES, None, None),
        P(AXES, None),
    )
    out_specs = (P(AXES, None, None), P(AXES, None))
    return jax.shard_map(
        per_device, mesh=mesh, in_specs=in_specs, out_specs=out_specs, check_vma=False
    )
```

```python
import functools

import jax
import jax.numpy as jnp
from jax import lax
from jax.experimental import pallas as pl
from jax.experimental.pallas import tpu as pltpu
from jax.sharding import PartitionSpec as P

exchange_coeff = 0.9847450218426964
AXES = ("row", "col")
VMEM_BYTES = 56 * 1024 * 1024
GROUP = 4
PARTS = 2


def fetch_kernel(asked_ref, tiles_ref, out_ref, flat_ref, sem):
    slots = out_ref.shape[0]

    def start(step, carry):
        for lane in range(16):
            slot = step * 16 + lane
            named = asked_ref[step * (16 // GROUP) + lane // GROUP, lane % GROUP]
            flat_ref[slot] = named
            tile = jnp.maximum(named, 0)
            pltpu.make_async_copy(tiles_ref.at[tile], out_ref.at[slot], sem).start()
        return carry

    lax.fori_loop(0, slots // 16, start, 0)
    pltpu.make_async_copy(out_ref, out_ref, sem).wait()


def region_kernel(
    slot_ref, values_ref, weights_ref, reply_ref, out_ref, density_ref,
    block, scaled, partial, store_sem,
):
    points, width_all = values_ref.shape
    width = reply_ref.shape[1]
    sig = width_all // width
    chunk = 4 * width
    chunks = width_all // chunk

    total = jnp.zeros((points, width), jnp.float32)
    for j in range(chunks):
        for q in range(4 * j, 4 * j + 4):
            for p in range(sig):
                block[q, pl.ds(p * width, width)] = reply_ref[slot_ref[p * sig + q]]
        columns = jnp.concatenate([block[4 * j + k] for k in range(4)], axis=1)
        mixed = jnp.dot(values_ref[...], columns, preferred_element_type=jnp.float32)
        product = mixed * values_ref[:, pl.ds(j * chunk, chunk)].astype(jnp.float32)
        total = total + sum(product[:, k * width:(k + 1) * width] for k in range(4))
    density = jnp.sum(total, axis=1, keepdims=True)
    density = jnp.broadcast_to(density, (points, width))
    density_ref[...] = density.T[:1, :]
    weights = jnp.broadcast_to(weights_ref[...], (width, points)).T
    cube_root = jnp.exp(jnp.log(density * density + 1.0) * (1.0 / 3.0))
    weighted = -exchange_coeff * weights * density / cube_root
    for q in range(sig):
        columns = pl.ds(q * width, width)
        scaled[:, columns] = (weighted * values_ref[:, columns].astype(jnp.float32)).astype(jnp.bfloat16)
    for i in range(chunks):
        rows = pl.ds(i * chunk, chunk)
        result = lax.dot_general(
            values_ref[:, rows], scaled[...], (((0,), (0,)), ((), ())), preferred_element_type=jnp.float32
        ).astype(jnp.bfloat16)
        for half in range(4):
            for q in range(sig):
                pair = (4 * i + half) * sig + q
                partial[pair] = result[half * width:(half + 1) * width, q * width:(q + 1) * width]
                pltpu.make_async_copy(partial.at[pair], out_ref.at[slot_ref[pair]], store_sem).start()
    pltpu.make_async_copy(partial, partial, store_sem).wait()


def collect_kernel(asked_ref, arrived_ref, out_ref, held, seen, sems):
    slots = arrived_ref.shape[0]
    stored, width = out_ref.shape[:2]
    parts = sems.shape[0]
    height = width // parts

    def forget(tile, carry):
        seen[tile] = 0
        return carry

    lax.fori_loop(0, stored + 1, forget, 0, unroll=8)

    def strip(part):
        rows = pl.ds(part * height, height)
        return pltpu.make_async_copy(held.at[pl.ds(0, stored), rows], out_ref.at[:, rows], sems.at[part])

    def clear(tile, carry):
        @pl.when(seen[tile] == 0)
        def _():
            held[tile] = jnp.zeros(held.shape[1:], jnp.float32)

        return carry

    for part in range(parts):
        rows = pl.ds(part * height, height)

        def add(group, carry):
            base = group * GROUP
            tiles = [asked_ref[base + k] for k in range(GROUP)]
            tiles = [jnp.where(tile < 0, stored, tile) for tile in tiles]
            kept = [seen[tile] > part for tile in tiles]
            sums = []
            for k in range(GROUP):
                before = held[tiles[k], rows]
                sums.append(jnp.where(kept[k], before, 0.0) + arrived_ref[base + k, rows].astype(jnp.float32))
            for k in range(GROUP):
                held[tiles[k], rows] = sums[k]
                seen[tiles[k]] = part + 1
            return carry

        lax.fori_loop(0, slots // GROUP, add, 0)
        if part == 0:
            lax.fori_loop(0, stored, clear, 0)
        strip(part).start()
    for part in range(parts):
        strip(part).wait()


def fetch(asked, tiles):
    slots = asked.shape[0] * GROUP
    return pl.pallas_call(
        fetch_kernel,
        out_shape=(
            jax.ShapeDtypeStruct((slots,) + tiles.shape[1:], tiles.dtype),
            jax.ShapeDtypeStruct((slots,), jnp.int32),
        ),
        in_specs=[pl.BlockSpec(memory_space=pltpu.SMEM), pl.BlockSpec(memory_space=pltpu.VMEM)],
        out_specs=(pl.BlockSpec(memory_space=pl.ANY), pl.BlockSpec(memory_space=pltpu.SMEM)),
        scratch_shapes=[pltpu.SemaphoreType.DMA],
        compiler_params=pltpu.CompilerParams(vmem_limit_bytes=VMEM_BYTES),
        name="fetch_tiles",
    )(asked, tiles)


def region(slot_of, values, weights, reply):
    points, width_all = values.shape
    width = reply.shape[1]
    vmem = pl.BlockSpec(memory_space=pltpu.VMEM)
    hbm = pl.BlockSpec(memory_space=pl.ANY)
    return pl.pallas_call(
        region_kernel,
        out_shape=(
            jax.ShapeDtypeStruct(reply.shape, jnp.bfloat16),
            jax.ShapeDtypeStruct((1, points), jnp.float32),
        ),
        in_specs=[pl.BlockSpec(memory_space=pltpu.SMEM), vmem, vmem, vmem],
        out_specs=(hbm, vmem),
        scratch_shapes=[
            pltpu.VMEM((width_all // width, width_all, width), jnp.bfloat16),
            pltpu.VMEM((points, width_all), jnp.bfloat16),
            pltpu.VMEM((slot_of.shape[0], width, width), jnp.bfloat16),
            pltpu.SemaphoreType.DMA,
        ],
        compiler_params=pltpu.CompilerParams(vmem_limit_bytes=34 * 1024 * 1024),
        name="region_work",
    )(slot_of, values, weights, reply)


def collect(asked, arrived, stored):
    return pl.pallas_call(
        collect_kernel,
        out_shape=jax.ShapeDtypeStruct((stored,) + arrived.shape[1:], jnp.float32),
        in_specs=[pl.BlockSpec(memory_space=pltpu.SMEM), pl.BlockSpec(memory_space=pltpu.VMEM)],
        out_specs=pl.BlockSpec(memory_space=pl.ANY),
        scratch_shapes=[
            pltpu.VMEM((stored + 1,) + arrived.shape[1:], jnp.float32),
            pltpu.SMEM((stored + 1,), jnp.int32),
            pltpu.SemaphoreType.DMA((PARTS,)),
        ],
        compiler_params=pltpu.CompilerParams(vmem_limit_bytes=20 * 1024 * 1024),
        name="collect_tiles",
    )(asked, arrived)


def per_device(basis_values, grid_weights, density_tiles, tile_index):
    devices = lax.axis_size("row") * lax.axis_size("col")
    stored = density_tiles.shape[0]
    pairs = tile_index.shape[1]
    capacity = 2 * pairs // devices
    exchange = functools.partial(
        lax.all_to_all, axis_name=AXES, split_axis=0, concat_axis=0, tiled=True
    )
    wanted = tile_index[0]
    owner_of = wanted // stored
    local_of = wanted % stored
    order_ids = jnp.arange(pairs, dtype=jnp.int32)
    earlier = order_ids[:, None] < order_ids[None, :]
    same_owner = owner_of[:, None] == owner_of[None, :]
    position = jnp.sum((same_owner & earlier).astype(jnp.int32), axis=0)
    slot_of = owner_of * capacity + position
    device_ids = jnp.arange(devices, dtype=jnp.int32)
    lanes = jnp.arange(stored, dtype=jnp.int32)
    to_owner = (owner_of[None, :] == device_ids[:, None]).astype(jnp.bfloat16)
    named = jnp.where(position[:, None] == lanes[None, :], (local_of + 1)[:, None], 0)
    send_local = jnp.dot(to_owner, named.astype(jnp.bfloat16), preferred_element_type=jnp.float32)
    asked = exchange(send_local.astype(jnp.int32) - 1)
    fetched, asked = fetch(asked, density_tiles)
    fetched, slot_of, asked = lax.optimization_barrier((fetched, slot_of, asked))
    reply = pltpu.with_memory_space_constraint(exchange(fetched), pltpu.VMEM)
    values = pltpu.with_memory_space_constraint(basis_values[0], pltpu.VMEM)
    outgoing, density = region(slot_of, values, grid_weights, reply)
    arrived = pltpu.with_memory_space_constraint(exchange(outgoing), pltpu.VMEM)
    return collect(asked, arrived, stored), density


def solution(mesh):
    in_specs = (
        P(AXES, None, None),
        P(AXES, None),
        P(AXES, None, None),
        P(AXES, None),
    )
    out_specs = (P(AXES, None, None), P(AXES, None))
    return jax.shard_map(
        per_device, mesh=mesh, in_specs=in_specs, out_specs=out_specs, check_vma=False
    )
```
